32 devices in a mesh: gx: 4 (over x, core), yz: 8 (over z, y).
Axes of the slice: x: 2, y: 2, z: 4, core: 2. Of those that a mesh axis runs over, the one named last changes fastest.
Arguments:
- right_side: float32 [3, 32, 1024, 256], P(None, 'gx', 'yz'), may hold values from -30 to 30
- viscosity: bfloat16 [32, 1024, 256], P('gx', 'yz'), may hold values from 0.29882812 to 3
- strain_rate: bfloat16 [6, 32, 1024, 256], P(None, 'gx', 'yz'), may hold values from -6 to 6
- cell_code: int32 [32, 1024, 256], P('gx', 'yz'), may hold values from 0 to 2
Outputs:
- solution_field: float32 [3, 32, 1024, 256], P(None, 'gx', 'yz')
- residual: float32 [3, 32, 1024, 256], P(None, 'gx', 'yz')
The draws below stay inside these ranges and needn't reach their ends.
All inputs are finite; a program needn't handle non-finite values.
Results may differ from the reference program's by a relative error of at most 0.0003.
Values may be sent and summed in bfloat16 or wider, within the bound.
A program may use at most 128 MiB of HBM per device.

```python
import math
import jax
import jax.numpy as jnp

ITERS = 3
NX = 32
NY = 1024
NZ = 256


def draw_right_side(key, part):
    keys = jax.random.split(key, 3)
    xpos = jnp.arange(NX, dtype=jnp.float32) / NX
    ypos = jnp.arange(NY, dtype=jnp.float32) / NY
    ramp = jnp.exp(jnp.log(3.0) * 0.5 * (xpos[:, None, None] + ypos[None, :, None]))
    value = jax.random.normal(keys[2], (3, NX, NY, NZ), jnp.float32) * ramp[None]
    return jnp.clip(value, -30.0, 30.0)


def place_ends(array, key, smallest, largest):
    longest = array.shape.index(max(array.shape))
    spots = []
    for shift in (0, 1):
        where = [jax.random.randint(jax.random.fold_in(key, axis), (), 0, length) for axis, length in enumerate(array.shape)]
        where[longest] = (where[longest] + shift) % array.shape[longest]
        spots.append(tuple(where))
    return array.at[spots[0]].set(smallest).at[spots[1]].set(largest)


def steps_of(stream_key, shape, cuts, smallest, high):
    gain, own = 1.0, jax.random.fold_in(stream_key, 6)
    for dim, shards_of in cuts:
        heights = jnp.exp(jax.random.uniform(jax.random.fold_in(own, dim), (shards_of,), jnp.float32, smallest / len(cuts), high / len(cuts)))
        gain = gain * jnp.repeat(heights, shape[dim] // shards_of).reshape([-1 if axis == dim else 1 for axis in range(len(shape))])
    return gain


def gaussian(own_key, dims, deviation, reach, pieces=(), kind=jnp.bfloat16):
    level = steps_of(own_key, dims, pieces, -0.22, 0.18) if pieces else 1.0
    values = jax.random.normal(own_key, dims, jnp.float32) * deviation * level
    return jnp.minimum(jnp.maximum(values, -reach), reach).astype(kind)


def setup_inputs(seed: int = 0) -> dict:
    splits = jax.random.split(jax.random.key(seed), 5)
    return {
        "right_side": draw_right_side(jax.random.fold_in(splits[4], 71), 0),
        "viscosity": jnp.clip(jnp.exp(math.log(3.0) - 2.306499 * jax.random.uniform(splits[1], (NX, NY, NZ), jnp.float32) ** steps_of(splits[1], (NX, NY, NZ), ((0, 4), (1, 8)), -0.2, 0.2)), 0.29882812, 3.0).astype(jnp.bfloat16),
        "strain_rate": gaussian(splits[2], (6, NX, NY, NZ), 1.0, 6.0, ((1, 4), (2, 8))),
        "cell_code": place_ends(jax.random.randint(splits[3], (NX, NY, NZ), 0, 3), jax.random.fold_in(splits[3], 1), 0, 2).astype(jnp.int32),
    }


SOFTEN = 0.8


def stresses(base, next_x, next_y, next_z, viscosity, strain_rate):
    along_x = next_x - base
    along_y = next_y - base
    along_z = next_z - base
    strain = strain_rate.astype(jnp.float32)
    two_eta = 2.0 * viscosity.astype(jnp.float32)
    parts = [along_x[0], along_y[1], along_z[2], 0.5 * (along_y[0] + along_x[1]), 0.5 * (along_z[0] + along_x[2]), 0.5 * (along_z[1] + along_y[2])]
    self_dot = strain[0] * strain[0] + strain[1] * strain[1] + strain[2] * strain[2] + 2.0 * (strain[3] * strain[3] + strain[4] * strain[4] + strain[5] * strain[5])
    cross_dot = strain[0] * parts[0] + strain[1] * parts[1] + strain[2] * parts[2] + 2.0 * (strain[3] * parts[3] + strain[4] * parts[4] + strain[5] * parts[5])
    factor = SOFTEN * cross_dot / (1.0 + self_dot)
    taus = [two_eta * (parts[k] - factor * strain[k]) for k in range(6)]
    flux_x = jnp.stack([taus[0], taus[3], taus[4]])
    flux_y = jnp.stack([taus[3], taus[1], taus[5]])
    flux_z = jnp.stack([taus[4], taus[5], taus[2]])
    return flux_x, flux_y, flux_z


def divergence(own_x, prev_x, own_y, prev_y, own_z, prev_z):
    return (prev_x - own_x) + (prev_y - own_y) + (prev_z - own_z)


def coefficients(cell_code):
    mask = (cell_code != 0).astype(jnp.float32)
    weight = jnp.where(cell_code == 0, 1.0, jnp.where(cell_code == 1, 0.2, 1.2)).astype(jnp.float32)
    return mask, weight


def operate(field, viscosity, strain_rate, mask, weight):
    masked = mask * field
    zero_x = jnp.zeros_like(masked[:, :1])
    zero_y = jnp.zeros_like(masked[:, :, :1])
    zero_z = jnp.zeros_like(masked[..., :1])
    next_x = jnp.concatenate([masked[:, 1:], zero_x], 1)
    next_y = jnp.concatenate([masked[:, :, 1:], zero_y], 2)
    next_z = jnp.concatenate([masked[..., 1:], zero_z], 3)
    flux_x, flux_y, flux_z = stresses(masked, next_x, next_y, next_z, viscosity, strain_rate)
    prev_x = jnp.concatenate([zero_x, flux_x[:, :-1]], 1)
    prev_y = jnp.concatenate([zero_y, flux_y[:, :, :-1]], 2)
    prev_z = jnp.concatenate([zero_z, flux_z[..., :-1]], 3)
    return mask * divergence(flux_x, prev_x, flux_y, prev_y, flux_z, prev_z) + weight * field


def reference(right_side, viscosity, strain_rate, cell_code):
    mask, weight = coefficients(cell_code)
    solution_field = jnp.zeros_like(right_side)
    residual = right_side
    direction = right_side
    norm_now = jnp.sum(residual * residual)
    for iteration in range(ITERS):
        image = operate(direction, viscosity, strain_rate, mask, weight)
        alpha = norm_now / jnp.sum(direction * image)
        solution_field = solution_field + alpha * direction
        residual = residual - alpha * image
        norm_next = jnp.sum(residual * residual)
        direction = residual + (norm_next / norm_now) * direction
        norm_now = norm_next
    return solution_field, residual
```

```python
import functools

import jax
import jax.numpy as jnp
from jax import lax
from jax.experimental import pallas as pl
from jax.experimental.pallas import tpu as pltpu
from jax.sharding import PartitionSpec as P

SOFTEN = 0.8
ROWS = 8
PACKED = 16
RING = 4
UNROLL = 2
MESH = pl.DeviceIdType.MESH

UP_X, DOWN_X, UP_DIAG, DOWN_DIAG, UP_Y, DOWN_Y = 0, 1, 2, 3, 4, 7
MESSAGES = 10
LOW, MID, HIGH = 0, 1, 2


def softening(strain, eta):
    self_dot = (
        strain[0] * strain[0] + strain[1] * strain[1] + strain[2] * strain[2]
        + 2.0 * (strain[3] * strain[3] + strain[4] * strain[4] + strain[5] * strain[5])
    )
    return (2.0 * SOFTEN) * eta / (1.0 + self_dot)


def stress(base, next_x, next_y, next_z, strain, eta, soft):
    along_x = [next_x[c] - base[c] for c in range(3)]
    along_y = [next_y[c] - base[c] for c in range(3)]
    along_z = [next_z[c] - base[c] for c in range(3)]
    parts = [
        along_x[0], along_y[1], along_z[2],
        along_y[0] + along_x[1], along_z[0] + along_x[2], along_z[1] + along_y[2],
    ]
    cross = (
        (strain[0] * parts[0] + strain[1] * parts[1])
        + (strain[2] * parts[2] + strain[3] * parts[3])
        + (strain[4] * parts[4] + strain[5] * parts[5])
    )
    factor = soft * cross
    twice = eta + eta
    return [(twice if k < 3 else eta) * parts[k] - factor * strain[k] for k in range(6)]


def kernel(
    gx_size, yz_size,
    load, viscosity, strain_rate, code,
    field, resid,
    m0, m1, m2, strain, eta, soft, weight, flux,
    raw_s, raw_v, raw_c, edge_xs, edge_xv, edge_ys, edge_yv,
    sums_x, sums_y,
    load_sem, raw_sem, send_sem, recv_sem, edge_send, edge_recv,
    sum_send_x, sum_recv_x, sum_send_y, sum_recv_y,
):
    _, X, Y, Z = load.shape
    blocks = Y // ROWS
    gx = lax.axis_index("gx")
    yz = lax.axis_index("yz")
    low_x, high_x = gx == 0, gx == gx_size - 1
    low_y, high_y = yz == 0, yz == yz_size - 1
    not_ = jnp.logical_not
    both = jnp.logical_and
    above_x, below_x = lax.rem(gx + 1, gx_size), lax.rem(gx + gx_size - 1, gx_size)
    above_y, below_y = lax.rem(yz + 1, yz_size), lax.rem(yz + yz_size - 1, yz_size)
    ring = min(RING, X)

    def layer_of(i):
        return lax.rem(i + X - 1, X)

    def load_copy(x):
        return pltpu.make_async_copy(load.at[:, x], field.at[:, x], load_sem.at[x])

    def raw_copies(i):
        x, slot = layer_of(i), lax.rem(i, ring)
        return (
            pltpu.make_async_copy(strain_rate.at[:, x], raw_s.at[slot], raw_sem.at[0, slot]),
            pltpu.make_async_copy(viscosity.at[x], raw_v.at[slot], raw_sem.at[1, slot]),
            pltpu.make_async_copy(code.at[x], raw_c.at[slot], raw_sem.at[2, slot]),
        )

    for i in range(ring):
        for copy in raw_copies(jnp.int32(i)):
            copy.start()
        load_copy(layer_of(jnp.int32(i))).start()
    for i in range(ring, X):
        load_copy(layer_of(jnp.int32(i))).start()

    barrier = pltpu.get_barrier_semaphore()
    for k in range(1, gx_size):
        pl.semaphore_signal(barrier, inc=1, device_id=(lax.rem(gx + k, gx_size), yz), device_id_type=MESH)
    for k in range(1, yz_size):
        pl.semaphore_signal(barrier, inc=1, device_id=(gx, lax.rem(yz + k, yz_size)), device_id_type=MESH)
    has_up_diag = both(not_(high_x), not_(low_y))
    has_down_diag = both(not_(low_x), not_(high_y))

    for peer in ((above_x, below_y), (below_x, above_y)):
        pl.semaphore_signal(barrier, inc=1, device_id=peer, device_id_type=MESH)

    fields = (m0, m1, m2)

    @pl.when(low_x)
    def _():
        strain[:, 0, ROWS:] = jnp.zeros((6, Y, Z), jnp.float32)
        eta[0, ROWS:] = jnp.zeros((Y, Z), jnp.float32)
        soft[0, ROWS:] = jnp.zeros((Y, Z), jnp.float32)
        for m in fields:
            m[:, 0, ROWS:] = jnp.zeros((3, Y + ROWS, Z), jnp.float32)

    @pl.when(high_x)
    def _():
        for m in fields:
            m[:, X + 1] = jnp.zeros((3, Y + 2 * ROWS, Z), jnp.float32)

    @pl.when(low_y)
    def _():
        strain[:, 1:, :ROWS] = jnp.zeros((6, X, ROWS, Z), jnp.float32)
        eta[1:, :ROWS] = jnp.zeros((X, ROWS, Z), jnp.float32)
        soft[1:, :ROWS] = jnp.zeros((X, ROWS, Z), jnp.float32)
        for m in fields:
            m[:, 1:, :ROWS] = jnp.zeros((3, X + 1, ROWS, Z), jnp.float32)

    @pl.when(high_y)
    def _():
        for m in fields:
            m[:, :X + 1, Y + ROWS:] = jnp.zeros((3, X + 1, ROWS, Z), jnp.float32)

    pl.semaphore_wait(barrier, gx_size - 1 + yz_size - 1 + 2)

    def edge(i):
        src, dst, to = (
            (strain_rate.at[:, X - 1], edge_xs, (above_x, yz)),
            (viscosity.at[X - 1], edge_xv, (above_x, yz)),
            (strain_rate.at[:, :, pl.ds(Y - PACKED, PACKED)], edge_ys, (gx, above_y)),
            (viscosity.at[:, pl.ds(Y - PACKED, PACKED)], edge_yv, (gx, above_y)),
        )[i]
        return pltpu.make_async_remote_copy(
            src_ref=src, dst_ref=dst, send_sem=edge_send.at[i], recv_sem=edge_recv.at[i],
            device_id=to, device_id_type=MESH,
        )

    @pl.when(not_(high_y))
    def _():
        edge(2).start()
        edge(3).start()

    sends = [not_(high_x), not_(low_x), has_up_diag, has_down_diag] + [not_(high_y)] * 3 + [not_(low_y)] * 3
    recvs = [not_(low_x), not_(high_x), has_down_diag, has_up_diag] + [not_(low_y)] * 3 + [not_(high_y)] * 3

    def message(step, i):
        m = fields[step]
        own = pl.ds(ROWS, Y)
        first, last = pl.ds(ROWS, ROWS), pl.ds(Y, ROWS)
        under, over = pl.ds(0, ROWS), pl.ds(Y + ROWS, ROWS)
        part = (pl.ds(1, 1), pl.ds(2, X - 2), pl.ds(X, 1))
        if i == UP_X:
            src, dst, to = m.at[:, X, own], m.at[:, 0, own], (above_x, yz)
        elif i == DOWN_X:
            src, dst, to = m.at[:, 1, own], m.at[:, X + 1, own], (below_x, yz)
        elif i == UP_DIAG:
            src, dst, to = m.at[:, X, first], m.at[:, 0, over], (above_x, below_y)
        elif i == DOWN_DIAG:
            src, dst, to = m.at[:, 1, last], m.at[:, X + 1, under], (below_x, above_y)
        elif i < DOWN_Y:
            src, dst, to = m.at[:, part[i - UP_Y], last], m.at[:, part[i - UP_Y], under], (gx, above_y)
        else:
            src, dst, to = m.at[:, part[i - DOWN_Y], first], m.at[:, part[i - DOWN_Y], over], (gx, below_y)
        return pltpu.make_async_remote_copy(
            src_ref=src, dst_ref=dst, send_sem=send_sem.at[step, i], recv_sem=recv_sem.at[step, i],
            device_id=to, device_id_type=MESH,
        )

    def send(step, which):
        for i in which:
            @pl.when(sends[i])
            def _(i=i):
                message(step, i).start()

    def receive(step, which):
        for i in which:
            @pl.when(recvs[i])
            def _(i=i):
                message(step, i).wait_recv()

    to_high = (UP_X, UP_DIAG, UP_Y + HIGH, DOWN_Y + HIGH)
    to_low = (DOWN_X, DOWN_DIAG, UP_Y + LOW, DOWN_Y + LOW)
    to_mid = (UP_Y + MID, DOWN_Y + MID)

    zero = jnp.zeros((ROWS, Z), jnp.float32)

    def prepare(i, sums):
        x, slot = layer_of(i), lax.rem(i, ring)
        for copy in raw_copies(i):
            copy.wait()
        load_copy(x).wait()

        def body(j, sums):
            held, free = sums
            here = pl.ds(pl.multiple_of(j * PACKED, PACKED), PACKED)
            there = pl.ds(pl.multiple_of(j * PACKED + ROWS, ROWS), PACKED)
            s = [raw_s[slot, k, here].astype(jnp.float32) for k in range(6)]
            v = raw_v[slot, here].astype(jnp.float32)
            kind = raw_c[slot, here]
            pin = kind == 0
            for k in range(6):
                strain[k, x + 1, there] = s[k]
            eta[x + 1, there] = v
            soft[x + 1, there] = softening(s, v)
            weight[x, here] = jnp.where(pin, 0.0, jnp.where(kind == 1, 0.2, 1.2)).astype(jnp.float32)
            for c in range(3):
                b = field[c, x, here]
                m = jnp.where(pin, 0.0, b)
                p = jnp.where(pin, b, 0.0)
                m0[c, x + 1, there] = m
                m, p = m * m, p * p
                free = free + (m[:ROWS] + m[ROWS:])
                held = held + (p[:ROWS] + p[ROWS:])
            return held, free

        sums = lax.fori_loop(0, Y // PACKED, body, sums)

        @pl.when(i + ring < X)
        def _():
            for copy in raw_copies(i + ring):
                copy.start()

        return sums

    sums = prepare(jnp.int32(0), (zero, zero))
    send(0, to_high)

    @pl.when(not_(high_x))
    def _():
        edge(0).start()
        edge(1).start()

    sums = prepare(jnp.int32(1), sums)
    send(0, to_low)
    held, free = lax.fori_loop(2, X, prepare, sums)
    send(0, to_mid)

    row = lax.broadcasted_iota(jnp.int32, (ROWS, Z), 0)
    lane = lax.broadcasted_iota(jnp.int32, (ROWS, Z), 1)
    top_row, bottom_row = row == 0, row == ROWS - 1
    first_lane, last_lane = lane == 0, lane == Z - 1

    def rows(j):
        return pl.ds(pl.multiple_of(j * ROWS, ROWS), ROWS)

    def tau(m, x, j, base, up):
        here = rows(j)
        next_x = [m[c, x + 1, here] for c in range(3)]
        next_y = [pltpu.roll(jnp.where(top_row, up[c], base[c]), ROWS - 1, 0) for c in range(3)]
        next_z = [jnp.where(last_lane, 0.0, pltpu.roll(base[c], Z - 1, 1)) for c in range(3)]
        s = [strain[k, x, here] for k in range(6)]
        return stress(base, next_x, next_y, next_z, s, eta[x, here], soft[x, here])

    def block(m, x, j):
        return tuple(m[c, x, rows(j)] for c in range(3))

    def flux_layer(m, x):
        def body(j, base):
            up = block(m, x, j + 1)
            t = tau(m, x, j, base, up)
            for c, k in enumerate((0, 3, 4)):
                flux[c, rows(j - 1)] = t[k]
            return up

        lax.fori_loop(1, blocks + 1, body, block(m, x, 1))

    def image_layer(m, out, shift, x, sums):
        base = block(m, x, 0)
        up = block(m, x, 1)
        t = tau(m, x, 0, base, up)

        def body(j, carry):
            base, prev, one, two = carry
            up = block(m, x, j + 1)
            t = tau(m, x, j, base, up)
            fx, fy, fz = (t[0], t[3], t[4]), (t[3], t[1], t[5]), (t[4], t[5], t[2])
            w = weight[x - 1, rows(j - 1)]
            kept = w > 0.0
            for c in range(3):
                before_x = flux[c, rows(j - 1)]
                before_y = pltpu.roll(jnp.where(bottom_row, prev[c], fy[c]), 1, 0)
                before_z = jnp.where(first_lane, 0.0, pltpu.roll(fz[c], 1, 1))
                value = (before_x - fx[c]) + (before_y - fy[c]) + (before_z - fz[c]) + w * base[c]
                value = jnp.where(kept, value, 0.0)
                flux[c, rows(j - 1)] = fx[c]
                out[c, x - shift, rows(j - shift)] = value
                one = one + base[c] * value
                two = two + value * value
            return up, fy, one, two

        carry = (up, (t[3], t[1], t[5])) + sums
        return lax.fori_loop(1, blocks + 1, body, carry, unroll=UNROLL)[2:]

    def edge_block(raw, shown, dst):
        s, v = raw
        s = [a.astype(jnp.float32)[shown] for a in s]
        v = v.astype(jnp.float32)[shown]
        x, at = dst
        for k in range(6):
            strain[k, x, at] = s[k]
        eta[x, at] = v
        soft[x, at] = softening(s, v)

    totals = [held, free]
    for step in range(3):
        m = fields[step]
        out, shift = (fields[step + 1], 0) if step < 2 else (resid, 1)
        receive(step, to_mid + (UP_Y + LOW, DOWN_Y + LOW, UP_Y + HIGH, DOWN_Y + HIGH))
        if step == 0:
            @pl.when(not_(low_y))
            def _():
                edge(2).wait_recv()
                edge(3).wait_recv()

                @pl.loop(0, X)
                def _(x):
                    raw = [edge_ys[k, x] for k in range(6)], edge_yv[x]
                    edge_block(raw, slice(PACKED - ROWS, PACKED), (x + 1, pl.ds(0, ROWS)))

        sums = (zero, zero)
        flux_layer(m, 1)
        sums = lax.fori_loop(2, X, functools.partial(image_layer, m, out, shift), sums)
        if step < 2:
            send(step + 1, to_mid)
        receive(step, (DOWN_X, DOWN_DIAG))
        sums = image_layer(m, out, shift, X, sums)
        if step < 2:
            send(step + 1, to_high)
        receive(step, (UP_X, UP_DIAG))
        if step == 0:
            @pl.when(not_(low_x))
            def _():
                edge(0).wait_recv()
                edge(1).wait_recv()

                @pl.loop(0, Y // PACKED)
                def _(j):
                    at = pl.ds(pl.multiple_of(j * PACKED, PACKED), PACKED)
                    raw = [edge_xs[k, at] for k in range(6)], edge_xv[at]
                    to = pl.ds(pl.multiple_of(j * PACKED + ROWS, ROWS), PACKED)
                    edge_block(raw, slice(0, PACKED), (0, to))

        flux_layer(m, 0)
        sums = image_layer(m, out, shift, 1, sums)
        if step < 2:
            send(step + 1, to_low)
        totals += list(sums)

    totals = totals[:7]
    lines = [sum(jnp.sum(a, 0, keepdims=True)[:, k:k + 128] for k in range(0, Z, 128)) for a in totals]
    number = lax.broadcasted_iota(jnp.int32, (8, 128), 0)
    tile = jnp.zeros((8, 128), jnp.float32)
    for k, line in enumerate(lines):
        tile = jnp.where(number == k, jnp.broadcast_to(line, (8, 128)), tile)

    def exchange(buf, axis, me, size, send_s, recv_s, tile):
        buf[me] = tile

        def copy(k):
            peer = lax.rem(me + k, size)
            to = (peer, yz) if axis == 0 else (gx, peer)
            return pltpu.make_async_remote_copy(
                src_ref=buf.at[me], dst_ref=buf.at[me], send_sem=send_s.at[k - 1],
                recv_sem=recv_s.at[k - 1], device_id=to, device_id_type=MESH,
            )

        def arrival(k):
            peer = lax.rem(me + size - k, size)
            to = (peer, yz) if axis == 0 else (gx, peer)
            return pltpu.make_async_remote_copy(
                src_ref=buf.at[peer], dst_ref=buf.at[peer], send_sem=send_s.at[k - 1],
                recv_sem=recv_s.at[k - 1], device_id=to, device_id_type=MESH,
            )

        for k in range(1, size):
            copy(k).start()
        for k in range(1, size):
            arrival(k).wait_recv()
        total = buf[0]
        for k in range(1, size):
            total = total + buf[k]
        for k in range(1, size):
            copy(k).wait_send()
        return total

    tile = exchange(sums_x, 0, gx, gx_size, sum_send_x, sum_recv_x, tile)
    tile = exchange(sums_y, 1, yz, yz_size, sum_send_y, sum_recv_y, tile)
    tile = jnp.sum(tile, axis=1, keepdims=True)
    pinned = tile[0:1]
    mu = [tile[k:k + 1] + pinned for k in range(1, 7)]

    scale = mu[1] / mu[0]
    n, power = [], jnp.ones_like(scale)
    for k in range(6):
        n.append(mu[k] / mu[0] / power)
        power = power * scale
    a11, a12, a22 = n[3] - n[2] * n[2], n[4] - n[2] * n[3], n[5] - n[3] * n[3]
    y1, y2 = 1.0 - n[2], n[2] - n[3]
    ratio = a12 / a11
    c2 = (y2 - ratio * y1) / (a22 - ratio * a12)
    c1 = (y1 - a12 * c2) / a11
    c0 = 1.0 - n[2] * c1 - n[3] * c2
    c0, c1, c2 = [
        jnp.broadcast_to(c, (ROWS, Z))
        for c in (c0 / scale, c1 / scale / scale, c2 / scale / scale / scale)
    ]

    @pl.loop(0, X)
    def _(x):
        @pl.loop(0, blocks)
        def _(j):
            here, there = rows(j), rows(j + 1)
            kept = weight[x, here] > 0.0
            for c in range(3):
                v0 = field[c, x, here]
                v1 = jnp.where(kept, m1[c, x + 1, there], v0)
                v2 = jnp.where(kept, m2[c, x + 1, there], v0)
                v3 = jnp.where(kept, resid[c, x, here], v0)
                field[c, x, here] = c0 * v0 + c1 * v1 + c2 * v2
                resid[c, x, here] = v0 - c0 * v1 - c1 * v2 - c2 * v3

    for step in range(3):
        for i in range(MESSAGES):
            @pl.when(sends[i])
            def _(step=step, i=i):
                message(step, i).wait_send()

    @pl.when(not_(high_x))
    def _():
        edge(0).wait_send()
        edge(1).wait_send()

    @pl.when(not_(high_y))
    def _():
        edge(2).wait_send()
        edge(3).wait_send()


def solution(mesh):
    gx_size, yz_size = mesh.shape["gx"], mesh.shape["yz"]

    def per_device(right_side, viscosity, strain_rate, cell_code):
        _, X, Y, Z = right_side.shape
        ring = min(RING, X)
        f32, bf16 = jnp.float32, jnp.bfloat16
        result = jax.ShapeDtypeStruct(right_side.shape, f32)
        padded = pltpu.VMEM((3, X + 2, Y + 2 * ROWS, Z), f32)
        dma = pltpu.SemaphoreType.DMA
        return pl.pallas_call(
            functools.partial(kernel, gx_size, yz_size),
            out_shape=(result, result),
            in_specs=[pl.BlockSpec(memory_space=pl.ANY)] * 4,
            out_specs=(pl.BlockSpec(memory_space=pltpu.VMEM),) * 2,
            scratch_shapes=[
                padded, padded, padded,
                pltpu.VMEM((6, X + 1, Y + ROWS, Z), f32),
                pltpu.VMEM((X + 1, Y + ROWS, Z), f32),
                pltpu.VMEM((X + 1, Y + ROWS, Z), f32),
                pltpu.VMEM((X, Y, Z), f32),
                pltpu.VMEM((3, Y, Z), f32),
                pltpu.VMEM((ring, 6, Y, Z), bf16),
                pltpu.VMEM((ring, Y, Z), bf16),
                pltpu.VMEM((ring, Y, Z), jnp.int32),
                pltpu.VMEM((6, Y, Z), bf16),
                pltpu.VMEM((Y, Z), bf16),
                pltpu.VMEM((6, X, PACKED, Z), bf16),
                pltpu.VMEM((X, PACKED, Z), bf16),
                pltpu.VMEM((gx_size, 8, 128), f32),
                pltpu.VMEM((yz_size, 8, 128), f32),
                dma((X,)), dma((3, ring)),
                dma((3, MESSAGES)), dma((3, MESSAGES)),
                dma((4,)), dma((4,)),
                dma((gx_size - 1,)), dma((gx_size - 1,)),
                dma((yz_size - 1,)), dma((yz_size - 1,)),
            ],
            compiler_params=pltpu.CompilerParams(
                collective_id=0, has_side_effects=True, vmem_limit_bytes=63 * 1024 * 1024,
            ),
        )(right_side, viscosity, strain_rate, cell_code)

    placed = (
        P(None, "gx", "yz", None),
        P("gx", "yz", None),
        P(None, "gx", "yz", None),
        P("gx", "yz", None),
    )
    return jax.shard_map(
        per_device,
        mesh=mesh,
        in_specs=placed,
        out_specs=(P(None, "gx", "yz", None), P(None, "gx", "yz", None)),
        check_vma=False,
    )
```

```python
import functools

import jax
import jax.numpy as jnp
from jax import lax
from jax.experimental import pallas as pl
from jax.experimental.pallas import tpu as pltpu
from jax.sharding import PartitionSpec as P

SOFTEN = 0.8
ROWS = 8
PACKED = 16
RING = 4
UNROLL = 4
MESH = pl.DeviceIdType.MESH

UP_X, DOWN_X, UP_DIAG, DOWN_DIAG, UP_Y, DOWN_Y = 0, 1, 2, 3, 4, 7
MESSAGES = 10
LOW, MID, HIGH = 0, 1, 2


def softening(strain, eta):
    self_dot = (
        strain[0] * strain[0] + strain[1] * strain[1] + strain[2] * strain[2]
        + 2.0 * (strain[3] * strain[3] + strain[4] * strain[4] + strain[5] * strain[5])
    )
    return (2.0 * SOFTEN) * eta / (1.0 + self_dot)


def stress(base, next_x, next_y, next_z, strain, eta, soft):
    along_x = [next_x[c] - base[c] for c in range(3)]
    along_y = [next_y[c] - base[c] for c in range(3)]
    along_z = [next_z[c] - base[c] for c in range(3)]
    parts = [
        along_x[0], along_y[1], along_z[2],
        along_y[0] + along_x[1], along_z[0] + along_x[2], along_z[1] + along_y[2],
    ]
    cross = (
        (strain[0] * parts[0] + strain[1] * parts[1])
        + (strain[2] * parts[2] + strain[3] * parts[3])
        + (strain[4] * parts[4] + strain[5] * parts[5])
    )
    factor = soft * cross
    twice = eta + eta
    return [(twice if k < 3 else eta) * parts[k] - factor * strain[k] for k in range(6)]


def kernel(
    gx_size, yz_size,
    load, viscosity, strain_rate, code,
    field, resid,
    m0, m1, m2, strain, eta, soft, weight, flux,
    raw_s, raw_v, raw_c, edge_xs, edge_xv, edge_ys, edge_yv,
    sums_x, sums_y,
    load_sem, raw_sem, send_sem, recv_sem, edge_send, edge_recv,
    sum_send_x, sum_recv_x, sum_send_y, sum_recv_y,
):
    _, X, Y, Z = load.shape
    blocks = Y // ROWS
    gx = lax.axis_index("gx")
    yz = lax.axis_index("yz")
    low_x, high_x = gx == 0, gx == gx_size - 1
    low_y, high_y = yz == 0, yz == yz_size - 1
    not_ = jnp.logical_not
    both = jnp.logical_and
    above_x, below_x = lax.rem(gx + 1, gx_size), lax.rem(gx + gx_size - 1, gx_size)
    above_y, below_y = lax.rem(yz + 1, yz_size), lax.rem(yz + yz_size - 1, yz_size)
    ring = min(RING, X)

    def layer_of(i):
        return lax.rem(i + X - 1, X)

    def load_copy(x):
        return pltpu.make_async_copy(load.at[:, x], field.at[:, x], load_sem.at[x])

    def raw_copies(i):
        x, slot = layer_of(i), lax.rem(i, ring)
        return (
            pltpu.make_async_copy(strain_rate.at[:, x], raw_s.at[slot], raw_sem.at[0, slot]),
            pltpu.make_async_copy(viscosity.at[x], raw_v.at[slot], raw_sem.at[1, slot]),
            pltpu.make_async_copy(code.at[x], raw_c.at[slot], raw_sem.at[2, slot]),
        )

    for i in range(ring):
        for copy in raw_copies(jnp.int32(i)):
            copy.start()
        load_copy(layer_of(jnp.int32(i))).start()
    for i in range(ring, X):
        load_copy(layer_of(jnp.int32(i))).start()

    barrier = pltpu.get_barrier_semaphore()
    for k in range(1, gx_size):
        pl.semaphore_signal(barrier, inc=1, device_id=(lax.rem(gx + k, gx_size), yz), device_id_type=MESH)
    for k in range(1, yz_size):
        pl.semaphore_signal(barrier, inc=1, device_id=(gx, lax.rem(yz + k, yz_size)), device_id_type=MESH)
    has_up_diag = both(not_(high_x), not_(low_y))
    has_down_diag = both(not_(low_x), not_(high_y))

    for peer in ((above_x, below_y), (below_x, above_y)):
        pl.semaphore_signal(barrier, inc=1, device_id=peer, device_id_type=MESH)

    fields = (m0, m1, m2)

    @pl.when(low_x)
    def _():
        strain[:, 0, ROWS:] = jnp.zeros((6, Y, Z), jnp.float32)
        eta[0, ROWS:] = jnp.zeros((Y, Z), jnp.float32)
        soft[0, ROWS:] = jnp.zeros((Y, Z), jnp.float32)
        for m in fields:
            m[:, 0, ROWS:] = jnp.zeros((3, Y + ROWS, Z), jnp.float32)

    @pl.when(high_x)
    def _():
        for m in fields:
            m[:, X + 1] = jnp.zeros((3, Y + 2 * ROWS, Z), jnp.float32)

    @pl.when(low_y)
    def _():
        strain[:, 1:, :ROWS] = jnp.zeros((6, X, ROWS, Z), jnp.float32)
        eta[1:, :ROWS] = jnp.zeros((X, ROWS, Z), jnp.float32)
        soft[1:, :ROWS] = jnp.zeros((X, ROWS, Z), jnp.float32)
        for m in fields:
            m[:, 1:, :ROWS] = jnp.zeros((3, X + 1, ROWS, Z), jnp.float32)

    @pl.when(high_y)
    def _():
        for m in fields:
            m[:, :X + 1, Y + ROWS:] = jnp.zeros((3, X + 1, ROWS, Z), jnp.float32)

    pl.semaphore_wait(barrier, gx_size - 1 + yz_size - 1 + 2)

    def edge(i):
        src, dst, to = (
            (strain_rate.at[:, X - 1], edge_xs, (above_x, yz)),
            (viscosity.at[X - 1], edge_xv, (above_x, yz)),
            (strain_rate.at[:, :, pl.ds(Y - PACKED, PACKED)], edge_ys, (gx, above_y)),
            (viscosity.at[:, pl.ds(Y - PACKED, PACKED)], edge_yv, (gx, above_y)),
        )[i]
        return pltpu.make_async_remote_copy(
            src_ref=src, dst_ref=dst, send_sem=edge_send.at[i], recv_sem=edge_recv.at[i],
            device_id=to, device_id_type=MESH,
        )

    @pl.when(not_(high_y))
    def _():
        edge(2).start()
        edge(3).start()

    sends = [not_(high_x), not_(low_x), has_up_diag, has_down_diag] + [not_(high_y)] * 3 + [not_(low_y)] * 3
    recvs = [not_(low_x), not_(high_x), has_down_diag, has_up_diag] + [not_(low_y)] * 3 + [not_(high_y)] * 3

    def message(step, i):
        m = fields[step]
        own = pl.ds(ROWS, Y)
        first, last = pl.ds(ROWS, ROWS), pl.ds(Y, ROWS)
        under, over = pl.ds(0, ROWS), pl.ds(Y + ROWS, ROWS)
        part = (pl.ds(1, 1), pl.ds(2, X - 2), pl.ds(X, 1))
        if i == UP_X:
            src, dst, to = m.at[:, X, own], m.at[:, 0, own], (above_x, yz)
        elif i == DOWN_X:
            src, dst, to = m.at[:, 1, own], m.at[:, X + 1, own], (below_x, yz)
        elif i == UP_DIAG:
            src, dst, to = m.at[:, X, first], m.at[:, 0, over], (above_x, below_y)
        elif i == DOWN_DIAG:
            src, dst, to = m.at[:, 1, last], m.at[:, X + 1, under], (below_x, above_y)
        elif i < DOWN_Y:
            src, dst, to = m.at[:, part[i - UP_Y], last], m.at[:, part[i - UP_Y], under], (gx, above_y)
        else:
            src, dst, to = m.at[:, part[i - DOWN_Y], first], m.at[:, part[i - DOWN_Y], over], (gx, below_y)
        return pltpu.make_async_remote_copy(
            src_ref=src, dst_ref=dst, send_sem=send_sem.at[step, i], recv_sem=recv_sem.at[step, i],
            device_id=to, device_id_type=MESH,
        )

    def send(step, which):
        for i in which:
            @pl.when(sends[i])
            def _(i=i):
                message(step, i).start()

    def receive(step, which):
        for i in which:
            @pl.when(recvs[i])
            def _(i=i):
                message(step, i).wait_recv()

    to_high = (UP_X, UP_DIAG, UP_Y + HIGH, DOWN_Y + HIGH)
    to_low = (DOWN_X, DOWN_DIAG, UP_Y + LOW, DOWN_Y + LOW)
    to_mid = (UP_Y + MID, DOWN_Y + MID)

    zero = jnp.zeros((ROWS, Z), jnp.float32)

    def prepare(i, sums):
        x, slot = layer_of(i), lax.rem(i, ring)
        for copy in raw_copies(i):
            copy.wait()
        load_copy(x).wait()

        def body(j, sums):
            held, free = sums
            here = pl.ds(pl.multiple_of(j * PACKED, PACKED), PACKED)
            there = pl.ds(pl.multiple_of(j * PACKED + ROWS, ROWS), PACKED)
            s = [raw_s[slot, k, here].astype(jnp.float32) for k in range(6)]
            v = raw_v[slot, here].astype(jnp.float32)
            kind = raw_c[slot, here]
            pin = kind == 0
            for k in range(6):
                strain[k, x + 1, there] = s[k]
            eta[x + 1, there] = v
            soft[x + 1, there] = softening(s, v)
            weight[x, here] = jnp.where(pin, 0.0, jnp.where(kind == 1, 0.2, 1.2)).astype(jnp.float32)
            for c in range(3):
                b = field[c, x, here]
                m = jnp.where(pin, 0.0, b)
                p = jnp.where(pin, b, 0.0)
                m0[c, x + 1, there] = m
                m, p = m * m, p * p
                free = free + (m[:ROWS] + m[ROWS:])
                held = held + (p[:ROWS] + p[ROWS:])
            return held, free

        sums = lax.fori_loop(0, Y // PACKED, body, sums, unroll=UNROLL)

        @pl.when(i + ring < X)
        def _():
            for copy in raw_copies(i + ring):
                copy.start()

        return sums

    sums = prepare(jnp.int32(0), (zero, zero))
    send(0, to_high)

    @pl.when(not_(high_x))
    def _():
        edge(0).start()
        edge(1).start()

    sums = prepare(jnp.int32(1), sums)
    send(0, to_low)
    held, free = lax.fori_loop(2, X, prepare, sums)
    send(0, to_mid)

    row = lax.broadcasted_iota(jnp.int32, (ROWS, Z), 0)
    lane = lax.broadcasted_iota(jnp.int32, (ROWS, Z), 1)
    top_row, bottom_row = row == 0, row == ROWS - 1
    first_lane, last_lane = lane == 0, lane == Z - 1

    def rows(j):
        return pl.ds(j * ROWS, ROWS)

    def tau(m, x, j, base, up):
        here = rows(j)
        next_x = [m[c, x + 1, here] for c in range(3)]
        next_y = [pltpu.roll(jnp.where(top_row, up[c], base[c]), ROWS - 1, 0) for c in range(3)]
        next_z = [jnp.where(last_lane, 0.0, pltpu.roll(base[c], Z - 1, 1)) for c in range(3)]
        s = [strain[k, x, here] for k in range(6)]
        return stress(base, next_x, next_y, next_z, s, eta[x, here], soft[x, here])

    def block(m, x, j):
        return tuple(m[c, x, rows(j)] for c in range(3))

    def flux_layer(m, x):
        base = block(m, x, 1)
        for j in range(1, blocks + 1):
            up = block(m, x, j + 1)
            t = tau(m, x, j, base, up)
            for c, k in enumerate((0, 3, 4)):
                flux[c, rows(j - 1)] = t[k]
            base = up

    def image_layer(m, out, shift, x, sums):
        one, two = sums
        base = block(m, x, 0)
        up = block(m, x, 1)
        t = tau(m, x, 0, base, up)
        base, prev = up, (t[3], t[1], t[5])
        for j in range(1, blocks + 1):
            up = block(m, x, j + 1)
            t = tau(m, x, j, base, up)
            fx, fy, fz = (t[0], t[3], t[4]), (t[3], t[1], t[5]), (t[4], t[5], t[2])
            w = weight[x - 1, rows(j - 1)]
            kept = w > 0.0
            for c in range(3):
                before_x = flux[c, rows(j - 1)]
                before_y = pltpu.roll(jnp.where(bottom_row, prev[c], fy[c]), 1, 0)
                before_z = jnp.where(first_lane, 0.0, pltpu.roll(fz[c], 1, 1))
                value = (before_x - fx[c]) + (before_y - fy[c]) + (before_z - fz[c]) + w * base[c]
                value = jnp.where(kept, value, 0.0)
                flux[c, rows(j - 1)] = fx[c]
                out[c, x - shift, rows(j - shift)] = value
                one = one + base[c] * value
                two = two + value * value
            base, prev = up, fy
        return one, two

    def edge_block(raw, shown, dst):
        s, v = raw
        s = [a.astype(jnp.float32)[shown] for a in s]
        v = v.astype(jnp.float32)[shown]
        x, at = dst
        for k in range(6):
            strain[k, x, at] = s[k]
        eta[x, at] = v
        soft[x, at] = softening(s, v)

    def coefficients_below():
        @pl.when(not_(low_x))
        def _():
            edge(0).wait_recv()
            edge(1).wait_recv()

            @pl.loop(0, Y // PACKED)
            def _(j):
                at = pl.ds(pl.multiple_of(j * PACKED, PACKED), PACKED)
                raw = [edge_xs[k, at] for k in range(6)], edge_xv[at]
                to = pl.ds(pl.multiple_of(j * PACKED + ROWS, ROWS), PACKED)
                edge_block(raw, slice(0, PACKED), (0, to))

    totals = [held, free]
    for step in range(3):
        m = fields[step]
        out, shift = (fields[step + 1], 0) if step < 2 else (resid, 1)
        receive(step, to_mid + (UP_Y + LOW, DOWN_Y + LOW, UP_Y + HIGH, DOWN_Y + HIGH))
        if step == 0:
            @pl.when(not_(low_y))
            def _():
                edge(2).wait_recv()
                edge(3).wait_recv()

                @pl.loop(0, X)
                def _(x):
                    raw = [edge_ys[k, x] for k in range(6)], edge_yv[x]
                    edge_block(raw, slice(PACKED - ROWS, PACKED), (x + 1, pl.ds(0, ROWS)))

        def turn(t, sums, step=step, m=m, out=out, shift=shift):
            x = lax.rem(t + 1, X) + 1

            @pl.when(t == X - 2)
            def _():
                if step < 2:
                    send(step + 1, to_mid)
                receive(step, (DOWN_X, DOWN_DIAG))

            @pl.when(t == X - 1)
            def _():
                if step < 2:
                    send(step + 1, to_high)
                receive(step, (UP_X, UP_DIAG))
                if step == 0:
                    coefficients_below()

            @pl.when(jnp.logical_or(t == 0, t == X - 1))
            def _():
                flux_layer(m, x - 1)

            return image_layer(m, out, shift, x, sums)

        sums = lax.fori_loop(0, X, turn, (zero, zero))
        if step < 2:
            send(step + 1, to_low)
        totals += list(sums)

    totals = totals[:7]
    lines = [sum(jnp.sum(a, 0, keepdims=True)[:, k:k + 128] for k in range(0, Z, 128)) for a in totals]
    number = lax.broadcasted_iota(jnp.int32, (8, 128), 0)
    tile = jnp.zeros((8, 128), jnp.float32)
    for k, line in enumerate(lines):
        tile = jnp.where(number == k, jnp.broadcast_to(line, (8, 128)), tile)

    def exchange(buf, axis, me, size, send_s, recv_s, tile):
        buf[me] = tile

        def copy(k):
            peer = lax.rem(me + k, size)
            to = (peer, yz) if axis == 0 else (gx, peer)
            return pltpu.make_async_remote_copy(
                src_ref=buf.at[me], dst_ref=buf.at[me], send_sem=send_s.at[k - 1],
                recv_sem=recv_s.at[k - 1], device_id=to, device_id_type=MESH,
            )

        def arrival(k):
            peer = lax.rem(me + size - k, size)
            to = (peer, yz) if axis == 0 else (gx, peer)
            return pltpu.make_async_remote_copy(
                src_ref=buf.at[peer], dst_ref=buf.at[peer], send_sem=send_s.at[k - 1],
                recv_sem=recv_s.at[k - 1], device_id=to, device_id_type=MESH,
            )

        for k in range(1, size):
            copy(k).start()
        for k in range(1, size):
            arrival(k).wait_recv()
        total = buf[0]
        for k in range(1, size):
            total = total + buf[k]
        for k in range(1, size):
            copy(k).wait_send()
        return total

    tile = exchange(sums_x, 0, gx, gx_size, sum_send_x, sum_recv_x, tile)
    tile = exchange(sums_y, 1, yz, yz_size, sum_send_y, sum_recv_y, tile)
    tile = jnp.sum(tile, axis=1, keepdims=True)
    pinned = tile[0:1]
    mu = [tile[k:k + 1] + pinned for k in range(1, 7)]

    scale = mu[1] / mu[0]
    n, power = [], jnp.ones_like(scale)
    for k in range(6):
        n.append(mu[k] / mu[0] / power)
        power = power * scale
    a11, a12, a22 = n[3] - n[2] * n[2], n[4] - n[2] * n[3], n[5] - n[3] * n[3]
    y1, y2 = 1.0 - n[2], n[2] - n[3]
    ratio = a12 / a11
    c2 = (y2 - ratio * y1) / (a22 - ratio * a12)
    c1 = (y1 - a12 * c2) / a11
    c0 = 1.0 - n[2] * c1 - n[3] * c2
    c0, c1, c2 = [
        jnp.broadcast_to(c, (ROWS, Z))
        for c in (c0 / scale, c1 / scale / scale, c2 / scale / scale / scale)
    ]

    @pl.loop(0, X)
    def _(x):
        for j in range(blocks):
            here, there = rows(j), rows(j + 1)
            kept = weight[x, here] > 0.0
            for c in range(3):
                v0 = field[c, x, here]
                v1 = jnp.where(kept, m1[c, x + 1, there], v0)
                v2 = jnp.where(kept, m2[c, x + 1, there], v0)
                v3 = jnp.where(kept, resid[c, x, here], v0)
                field[c, x, here] = c0 * v0 + c1 * v1 + c2 * v2
                resid[c, x, here] = v0 - c0 * v1 - c1 * v2 - c2 * v3

    for step in range(3):
        for i in range(MESSAGES):
            @pl.when(sends[i])
            def _(step=step, i=i):
                message(step, i).wait_send()

    @pl.when(not_(high_x))
    def _():
        edge(0).wait_send()
        edge(1).wait_send()

    @pl.when(not_(high_y))
    def _():
        edge(2).wait_send()
        edge(3).wait_send()


def solution(mesh):
    gx_size, yz_size = mesh.shape["gx"], mesh.shape["yz"]

    def per_device(right_side, viscosity, strain_rate, cell_code):
        _, X, Y, Z = right_side.shape
        ring = min(RING, X)
        f32, bf16 = jnp.float32, jnp.bfloat16
        result = pltpu.VMEM(right_side.shape, f32)
        padded = pltpu.VMEM((3, X + 2, Y + 2 * ROWS, Z), f32)
        dma = pltpu.SemaphoreType.DMA
        return pl.pallas_call(
            functools.partial(kernel, gx_size, yz_size),
            out_shape=(result, result),
            in_specs=[pl.BlockSpec(memory_space=pl.ANY)] * 4,
            out_specs=(pl.BlockSpec(memory_space=pltpu.VMEM),) * 2,
            scratch_shapes=[
                padded, padded, padded,
                pltpu.VMEM((6, X + 1, Y + ROWS, Z), f32),
                pltpu.VMEM((X + 1, Y + ROWS, Z), f32),
                pltpu.VMEM((X + 1, Y + ROWS, Z), f32),
                pltpu.VMEM((X, Y, Z), f32),
                pltpu.VMEM((3, Y, Z), f32),
                pltpu.VMEM((ring, 6, Y, Z), bf16),
                pltpu.VMEM((ring, Y, Z), bf16),
                pltpu.VMEM((ring, Y, Z), jnp.int32),
                pltpu.VMEM((6, Y, Z), bf16),
                pltpu.VMEM((Y, Z), bf16),
                pltpu.VMEM((6, X, PACKED, Z), bf16),
                pltpu.VMEM((X, PACKED, Z), bf16),
                pltpu.VMEM((gx_size, 8, 128), f32),
                pltpu.VMEM((yz_size, 8, 128), f32),
                dma((X,)), dma((3, ring)),
                dma((3, MESSAGES)), dma((3, MESSAGES)),
                dma((4,)), dma((4,)),
                dma((gx_size - 1,)), dma((gx_size - 1,)),
                dma((yz_size - 1,)), dma((yz_size - 1,)),
            ],
            compiler_params=pltpu.CompilerParams(
                collective_id=0, has_side_effects=True, vmem_limit_bytes=50 * 1024 * 1024,
            ),
        )(right_side, viscosity, strain_rate, cell_code)

    placed = (
        P(None, "gx", "yz", None),
        P("gx", "yz", None),
        P(None, "gx", "yz", None),
        P("gx", "yz", None),
    )
    return jax.shard_map(
        per_device,
        mesh=mesh,
        in_specs=placed,
        out_specs=(P(None, "gx", "yz", None), P(None, "gx", "yz", None)),
        check_vma=False,
    )
```

```python
import functools

import jax
import jax.numpy as jnp
from jax import lax
from jax.experimental import pallas as pl
from jax.experimental.pallas import tpu as pltpu
from jax.sharding import PartitionSpec as P

SOFTEN = 0.8
ROWS = 8
PACKED = 16
RING = 4
UNROLL = 4
MESH = pl.DeviceIdType.MESH

UP_X, DOWN_X, UP_DIAG, DOWN_DIAG, UP_MID, DOWN_MID, UP_ENDS, DOWN_ENDS = range(8)
MESSAGES = 8


def softening(strain, eta):
    self_dot = (
        strain[0] * strain[0] + strain[1] * strain[1] + strain[2] * strain[2]
        + 2.0 * (strain[3] * strain[3] + strain[4] * strain[4] + strain[5] * strain[5])
    )
    return (2.0 * SOFTEN) * eta / (1.0 + self_dot)


def stress(base, next_x, next_y, next_z, strain, eta, soft):
    along_x = [next_x[c] - base[c] for c in range(3)]
    along_y = [next_y[c] - base[c] for c in range(3)]
    along_z = [next_z[c] - base[c] for c in range(3)]
    parts = [
        along_x[0], along_y[1], along_z[2],
        along_y[0] + along_x[1], along_z[0] + along_x[2], along_z[1] + along_y[2],
    ]
    cross = (
        (strain[0] * parts[0] + strain[1] * parts[1])
        + (strain[2] * parts[2] + strain[3] * parts[3])
        + (strain[4] * parts[4] + strain[5] * parts[5])
    )
    factor = soft * cross
    twice = eta + eta
    return [(twice if k < 3 else eta) * parts[k] - factor * strain[k] for k in range(6)]


def kernel(
    gx_size, yz_size,
    load, viscosity, strain_rate, code,
    field, resid,
    m0, m1, m2, strain, eta, soft, weight, flux,
    raw_s, raw_v, raw_c, edge_xs, edge_xv, edge_out, edge_in,
    mid_out, mid_in, ends_out, ends_in,
    sums_x, sums_y,
    load_sem, raw_sem, send_sem, recv_sem, edge_send, edge_recv,
    sum_send_x, sum_recv_x, sum_send_y, sum_recv_y,
):
    _, X, Y, Z = load.shape
    blocks = Y // ROWS
    gx = lax.axis_index("gx")
    yz = lax.axis_index("yz")
    low_x, high_x = gx == 0, gx == gx_size - 1
    low_y, high_y = yz == 0, yz == yz_size - 1
    not_ = jnp.logical_not
    both = jnp.logical_and
    above_x, below_x = lax.rem(gx + 1, gx_size), lax.rem(gx + gx_size - 1, gx_size)
    above_y, below_y = lax.rem(yz + 1, yz_size), lax.rem(yz + yz_size - 1, yz_size)
    ring = min(RING, X)

    def layer_of(i):
        return lax.rem(i + X - 1, X)

    def load_copy(x):
        return pltpu.make_async_copy(load.at[:, x], field.at[:, x], load_sem.at[x])

    def raw_copies(i):
        x, slot = layer_of(i), lax.rem(i, ring)
        return (
            pltpu.make_async_copy(strain_rate.at[:, x], raw_s.at[slot], raw_sem.at[0, slot]),
            pltpu.make_async_copy(viscosity.at[x], raw_v.at[slot], raw_sem.at[1, slot]),
            pltpu.make_async_copy(code.at[x], raw_c.at[slot], raw_sem.at[2, slot]),
        )

    for i in range(ring):
        for copy in raw_copies(jnp.int32(i)):
            copy.start()
        load_copy(layer_of(jnp.int32(i))).start()
    for i in range(ring, X):
        load_copy(layer_of(jnp.int32(i))).start()

    barrier = pltpu.get_barrier_semaphore()
    for k in range(1, gx_size):
        pl.semaphore_signal(barrier, inc=1, device_id=(lax.rem(gx + k, gx_size), yz), device_id_type=MESH)
    for k in range(1, yz_size):
        pl.semaphore_signal(barrier, inc=1, device_id=(gx, lax.rem(yz + k, yz_size)), device_id_type=MESH)
    has_up_diag = both(not_(high_x), not_(low_y))
    has_down_diag = both(not_(low_x), not_(high_y))

    for peer in ((above_x, below_y), (below_x, above_y)):
        pl.semaphore_signal(barrier, inc=1, device_id=peer, device_id_type=MESH)

    fields = (m0, m1, m2)

    @pl.when(low_x)
    def _():
        strain[:, 0, ROWS:] = jnp.zeros((6, Y, Z), jnp.float32)
        eta[0, ROWS:] = jnp.zeros((Y, Z), jnp.float32)
        soft[0, ROWS:] = jnp.zeros((Y, Z), jnp.float32)
        for m in fields:
            m[:, 0, ROWS:] = jnp.zeros((3, Y + ROWS, Z), jnp.float32)

    @pl.when(high_x)
    def _():
        for m in fields:
            m[:, X + 1] = jnp.zeros((3, Y + 2 * ROWS, Z), jnp.float32)

    @pl.when(low_y)
    def _():
        strain[:, 1:, :ROWS] = jnp.zeros((6, X, ROWS, Z), jnp.float32)
        eta[1:, :ROWS] = jnp.zeros((X, ROWS, Z), jnp.float32)
        soft[1:, :ROWS] = jnp.zeros((X, ROWS, Z), jnp.float32)
        for m in fields:
            m[:, 1:, :ROWS] = jnp.zeros((3, X + 1, ROWS, Z), jnp.float32)

    @pl.when(high_y)
    def _():
        for m in fields:
            m[:, :X + 1, Y + ROWS:] = jnp.zeros((3, X + 1, ROWS, Z), jnp.float32)

    pl.semaphore_wait(barrier, gx_size - 1 + yz_size - 1 + 2)

    def edge(i):
        src, dst, to = (
            (strain_rate.at[:, X - 1], edge_xs, (above_x, yz)),
            (viscosity.at[X - 1], edge_xv, (above_x, yz)),
            (edge_out, edge_in, (gx, above_y)),
        )[i]
        return pltpu.make_async_remote_copy(
            src_ref=src, dst_ref=dst, send_sem=edge_send.at[i], recv_sem=edge_recv.at[i],
            device_id=to, device_id_type=MESH,
        )

    sends = [not_(high_x), not_(low_x), has_up_diag, has_down_diag] + [not_(high_y), not_(low_y)] * 2
    recvs = [not_(low_x), not_(high_x), has_down_diag, has_up_diag] + [not_(low_y), not_(high_y)] * 2

    def message(step, i):
        m = fields[step]
        own = pl.ds(ROWS, Y)
        first, last = pl.ds(ROWS, ROWS), pl.ds(Y, ROWS)
        under, over = pl.ds(0, ROWS), pl.ds(Y + ROWS, ROWS)
        if i == UP_X:
            src, dst, to = m.at[:, X, own], m.at[:, 0, own], (above_x, yz)
        elif i == DOWN_X:
            src, dst, to = m.at[:, 1, own], m.at[:, X + 1, own], (below_x, yz)
        elif i == UP_DIAG:
            src, dst, to = m.at[:, X, first], m.at[:, 0, over], (above_x, below_y)
        elif i == DOWN_DIAG:
            src, dst, to = m.at[:, 1, last], m.at[:, X + 1, under], (below_x, above_y)
        else:
            way = (i - UP_MID) % 2
            there, here = (mid_out, mid_in) if i < UP_ENDS else (ends_out, ends_in)
            src, dst = there.at[step, way], here.at[step, way]
            to = (gx, below_y if way else above_y)
        return pltpu.make_async_remote_copy(
            src_ref=src, dst_ref=dst, send_sem=send_sem.at[step, i], recv_sem=recv_sem.at[step, i],
            device_id=to, device_id_type=MESH,
        )

    def send(step, which):
        for i in which:
            @pl.when(sends[i])
            def _(i=i):
                message(step, i).start()

    def receive(step, which):
        for i in which:
            @pl.when(recvs[i])
            def _(i=i):
                message(step, i).wait_recv()

    to_high = (UP_X, UP_DIAG)
    to_low = (DOWN_X, DOWN_DIAG, UP_ENDS, DOWN_ENDS)
    to_mid = (UP_MID, DOWN_MID)

    def stage(step, x):
        m = fields[step]
        inner = both(x > 1, x < X)
        for way, at in enumerate((Y + ROWS - 1, ROWS)):
            line = [m[c, x, pl.ds(at, 1)] for c in range(3)]

            @pl.when(inner)
            def _(way=way, line=line):
                for c in range(3):
                    mid_out[step, way, c, pl.ds(x - 1, 1)] = line[c]

            @pl.when(x == 1)
            def _(way=way, line=line):
                for c in range(3):
                    ends_out[step, way, pl.ds(c, 1)] = line[c]

            @pl.when(x == X)
            def _(way=way, line=line):
                for c in range(3):
                    ends_out[step, way, pl.ds(3 + c, 1)] = line[c]

    def spread(step):
        m = fields[step]
        for way, at in enumerate((0, Y + ROWS)):
            @pl.when(recvs[UP_MID + way])
            def _(way=way, at=at):
                message(step, UP_MID + way).wait_recv()
                for c in range(3):
                    for x in range(2, X):
                        line = mid_in[step, way, c, pl.ds(x - 1, 1)]
                        m[c, x, pl.ds(at, ROWS)] = jnp.broadcast_to(line, (ROWS, Z))
                message(step, UP_ENDS + way).wait_recv()
                for c in range(3):
                    for k, x in ((0, 1), (3, X)):
                        line = ends_in[step, way, pl.ds(k + c, 1)]
                        m[c, x, pl.ds(at, ROWS)] = jnp.broadcast_to(line, (ROWS, Z))

    zero = jnp.zeros((ROWS, Z), jnp.float32)

    def prepare(i, sums):
        x, slot = layer_of(i), lax.rem(i, ring)
        for copy in raw_copies(i):
            copy.wait()
        load_copy(x).wait()

        def body(j, sums):
            held, free = sums
            here = pl.ds(pl.multiple_of(j * PACKED, PACKED), PACKED)
            there = pl.ds(pl.multiple_of(j * PACKED + ROWS, ROWS), PACKED)
            s = [raw_s[slot, k, here].astype(jnp.float32) for k in range(6)]
            v = raw_v[slot, here].astype(jnp.float32)
            kind = raw_c[slot, here]
            pin = kind == 0
            for k in range(6):
                strain[k, x + 1, there] = s[k]
            eta[x + 1, there] = v
            soft[x + 1, there] = softening(s, v)
            weight[x, here] = jnp.where(pin, 0.0, jnp.where(kind == 1, 0.2, 1.2)).astype(jnp.float32)
            for c in range(3):
                b = field[c, x, here]
                m = jnp.where(pin, 0.0, b)
                p = jnp.where(pin, b, 0.0)
                m0[c, x + 1, there] = m
                m, p = m * m, p * p
                free = free + (m[:ROWS] + m[ROWS:])
                held = held + (p[:ROWS] + p[ROWS:])
            return held, free

        sums = lax.fori_loop(0, Y // PACKED, body, sums, unroll=UNROLL)

        stage(0, x + 1)
        at = pl.ds(Y + ROWS - 1, 1)
        for k in range(6):
            edge_out[k, pl.ds(x, 1)] = strain[k, x + 1, at]
        edge_out[6, pl.ds(x, 1)] = eta[x + 1, at]
        edge_out[7, pl.ds(x, 1)] = soft[x + 1, at]

        @pl.when(i + ring < X)
        def _():
            for copy in raw_copies(i + ring):
                copy.start()

        return sums

    sums = prepare(jnp.int32(0), (zero, zero))
    send(0, to_high)

    @pl.when(not_(high_x))
    def _():
        edge(0).start()
        edge(1).start()

    sums = prepare(jnp.int32(1), sums)
    send(0, to_low)
    held, free = lax.fori_loop(2, X, prepare, sums)
    send(0, to_mid)

    @pl.when(not_(high_y))
    def _():
        edge(2).start()

    row = lax.broadcasted_iota(jnp.int32, (ROWS, Z), 0)
    lane = lax.broadcasted_iota(jnp.int32, (ROWS, Z), 1)
    top_row, bottom_row = row == 0, row == ROWS - 1
    first_lane, last_lane = lane == 0, lane == Z - 1

    def rows(j):
        return pl.ds(j * ROWS, ROWS)

    def tau(m, x, j, base, up):
        here = rows(j)
        next_x = [m[c, x + 1, here] for c in range(3)]
        next_y = [pltpu.roll(jnp.where(top_row, up[c], base[c]), ROWS - 1, 0) for c in range(3)]
        next_z = [jnp.where(last_lane, 0.0, pltpu.roll(base[c], Z - 1, 1)) for c in range(3)]
        s = [strain[k, x, here] for k in range(6)]
        return stress(base, next_x, next_y, next_z, s, eta[x, here], soft[x, here])

    def block(m, x, j):
        return tuple(m[c, x, rows(j)] for c in range(3))

    def flux_layer(m, x):
        base = block(m, x, 1)
        for j in range(1, blocks + 1):
            up = block(m, x, j + 1)
            t = tau(m, x, j, base, up)
            for c, k in enumerate((0, 3, 4)):
                flux[c, rows(j - 1)] = t[k]
            base = up

    def image_layer(m, out, shift, x, sums):
        one, two = sums
        base = block(m, x, 0)
        up = block(m, x, 1)
        t = tau(m, x, 0, base, up)
        base, prev = up, (t[3], t[1], t[5])
        for j in range(1, blocks + 1):
            up = block(m, x, j + 1)
            t = tau(m, x, j, base, up)
            fx, fy, fz = (t[0], t[3], t[4]), (t[3], t[1], t[5]), (t[4], t[5], t[2])
            w = weight[x - 1, rows(j - 1)]
            kept = w > 0.0
            for c in range(3):
                before_x = flux[c, rows(j - 1)]
                before_y = pltpu.roll(jnp.where(bottom_row, prev[c], fy[c]), 1, 0)
                before_z = jnp.where(first_lane, 0.0, pltpu.roll(fz[c], 1, 1))
                value = (before_x - fx[c]) + (before_y - fy[c]) + (before_z - fz[c]) + w * base[c]
                value = jnp.where(kept, value, 0.0)
                flux[c, rows(j - 1)] = fx[c]
                out[c, x - shift, rows(j - shift)] = value
                one = one + base[c] * value
                two = two + value * value
            base, prev = up, fy
        return one, two

    def edge_block(raw, shown, dst):
        s, v = raw
        s = [a.astype(jnp.float32)[shown] for a in s]
        v = v.astype(jnp.float32)[shown]
        x, at = dst
        for k in range(6):
            strain[k, x, at] = s[k]
        eta[x, at] = v
        soft[x, at] = softening(s, v)

    def coefficients_below():
        @pl.when(not_(low_x))
        def _():
            edge(0).wait_recv()
            edge(1).wait_recv()

            @pl.loop(0, Y // PACKED)
            def _(j):
                at = pl.ds(pl.multiple_of(j * PACKED, PACKED), PACKED)
                raw = [edge_xs[k, at] for k in range(6)], edge_xv[at]
                to = pl.ds(pl.multiple_of(j * PACKED + ROWS, ROWS), PACKED)
                edge_block(raw, slice(0, PACKED), (0, to))

    totals = [held, free]
    for step in range(3):
        m = fields[step]
        out, shift = (fields[step + 1], 0) if step < 2 else (resid, 1)
        spread(step)
        if step == 0:
            @pl.when(not_(low_y))
            def _():
                edge(2).wait_recv()
                for x in range(X):
                    line = [jnp.broadcast_to(edge_in[k, pl.ds(x, 1)], (ROWS, Z)) for k in range(8)]
                    for k in range(6):
                        strain[k, x + 1, pl.ds(0, ROWS)] = line[k]
                    eta[x + 1, pl.ds(0, ROWS)] = line[6]
                    soft[x + 1, pl.ds(0, ROWS)] = line[7]

        def turn(t, sums, step=step, m=m, out=out, shift=shift):
            x = lax.rem(t + 1, X) + 1

            @pl.when(t == X - 2)
            def _():
                if step < 2:
                    send(step + 1, to_mid)
                receive(step, (DOWN_X, DOWN_DIAG))

            @pl.when(t == X - 1)
            def _():
                if step < 2:
                    send(step + 1, to_high)
                receive(step, (UP_X, UP_DIAG))
                if step == 0:
                    coefficients_below()

            @pl.when(jnp.logical_or(t == 0, t == X - 1))
            def _():
                flux_layer(m, x - 1)

            sums = image_layer(m, out, shift, x, sums)
            if step < 2:
                stage(step + 1, x)
            return sums

        sums = lax.fori_loop(0, X, turn, (zero, zero))
        if step < 2:
            send(step + 1, to_low)
        totals += list(sums)

    totals = totals[:7]
    lines = [sum(jnp.sum(a, 0, keepdims=True)[:, k:k + 128] for k in range(0, Z, 128)) for a in totals]
    number = lax.broadcasted_iota(jnp.int32, (8, 128), 0)
    tile = jnp.zeros((8, 128), jnp.float32)
    for k, line in enumerate(lines):
        tile = jnp.where(number == k, jnp.broadcast_to(line, (8, 128)), tile)

    def exchange(buf, axis, me, size, send_s, recv_s, tile):
        buf[me] = tile

        def copy(k):
            peer = lax.rem(me + k, size)
            to = (peer, yz) if axis == 0 else (gx, peer)
            return pltpu.make_async_remote_copy(
                src_ref=buf.at[me], dst_ref=buf.at[me], send_sem=send_s.at[k - 1],
                recv_sem=recv_s.at[k - 1], device_id=to, device_id_type=MESH,
            )

        def arrival(k):
            peer = lax.rem(me + size - k, size)
            to = (peer, yz) if axis == 0 else (gx, peer)
            return pltpu.make_async_remote_copy(
                src_ref=buf.at[peer], dst_ref=buf.at[peer], send_sem=send_s.at[k - 1],
                recv_sem=recv_s.at[k - 1], device_id=to, device_id_type=MESH,
            )

        for k in range(1, size):
            copy(k).start()
        for k in range(1, size):
            arrival(k).wait_recv()
        total = buf[0]
        for k in range(1, size):
            total = total + buf[k]
        for k in range(1, size):
            copy(k).wait_send()
        return total

    tile = exchange(sums_x, 0, gx, gx_size, sum_send_x, sum_recv_x, tile)
    tile = exchange(sums_y, 1, yz, yz_size, sum_send_y, sum_recv_y, tile)
    tile = jnp.sum(tile, axis=1, keepdims=True)
    pinned = tile[0:1]
    mu = [tile[k:k + 1] + pinned for k in range(1, 7)]

    scale = mu[1] / mu[0]
    n, power = [], jnp.ones_like(scale)
    for k in range(6):
        n.append(mu[k] / mu[0] / power)
        power = power * scale
    a11, a12, a22 = n[3] - n[2] * n[2], n[4] - n[2] * n[3], n[5] - n[3] * n[3]
    y1, y2 = 1.0 - n[2], n[2] - n[3]
    ratio = a12 / a11
    c2 = (y2 - ratio * y1) / (a22 - ratio * a12)
    c1 = (y1 - a12 * c2) / a11
    c0 = 1.0 - n[2] * c1 - n[3] * c2
    c0, c1, c2 = [
        jnp.broadcast_to(c, (ROWS, Z))
        for c in (c0 / scale, c1 / scale / scale, c2 / scale / scale / scale)
    ]

    @pl.loop(0, X)
    def _(x):
        for j in range(blocks):
            here, there = rows(j), rows(j + 1)
            kept = weight[x, here] > 0.0
            for c in range(3):
                v0 = field[c, x, here]
                v1 = jnp.where(kept, m1[c, x + 1, there], v0)
                v2 = jnp.where(kept, m2[c, x + 1, there], v0)
                v3 = jnp.where(kept, resid[c, x, here], v0)
                field[c, x, here] = c0 * v0 + c1 * v1 + c2 * v2
                resid[c, x, here] = v0 - c0 * v1 - c1 * v2 - c2 * v3

    for step in range(3):
        for i in range(MESSAGES):
            @pl.when(sends[i])
            def _(step=step, i=i):
                message(step, i).wait_send()

    @pl.when(not_(high_x))
    def _():
        edge(0).wait_send()
        edge(1).wait_send()

    @pl.when(not_(high_y))
    def _():
        edge(2).wait_send()


def solution(mesh):
    gx_size, yz_size = mesh.shape["gx"], mesh.shape["yz"]

    def per_device(right_side, viscosity, strain_rate, cell_code):
        _, X, Y, Z = right_side.shape
        ring = min(RING, X)
        f32, bf16 = jnp.float32, jnp.bfloat16
        result = pltpu.VMEM(right_side.shape, f32)
        padded = pltpu.VMEM((3, X + 2, Y + 2 * ROWS, Z), f32)
        dma = pltpu.SemaphoreType.DMA
        return pl.pallas_call(
            functools.partial(kernel, gx_size, yz_size),
            out_shape=(result, result),
            in_specs=[pl.BlockSpec(memory_space=pl.ANY)] * 4,
            out_specs=(pl.BlockSpec(memory_space=pltpu.VMEM),) * 2,
            scratch_shapes=[
                padded, padded, padded,
                pltpu.VMEM((6, X + 1, Y + ROWS, Z), f32),
                pltpu.VMEM((X + 1, Y + ROWS, Z), f32),
                pltpu.VMEM((X + 1, Y + ROWS, Z), f32),
                pltpu.VMEM((X, Y, Z), f32),
                pltpu.VMEM((3, Y, Z), f32),
                pltpu.VMEM((ring, 6, Y, Z), bf16),
                pltpu.VMEM((ring, Y, Z), bf16),
                pltpu.VMEM((ring, Y, Z), jnp.int32),
                pltpu.VMEM((6, Y, Z), bf16),
                pltpu.VMEM((Y, Z), bf16),
                pltpu.VMEM((8, X, Z), f32), pltpu.VMEM((8, X, Z), f32),
                pltpu.VMEM((3, 2, 3, X, Z), f32), pltpu.VMEM((3, 2, 3, X, Z), f32),
                pltpu.VMEM((3, 2, 8, Z), f32), pltpu.VMEM((3, 2, 8, Z), f32),
                pltpu.VMEM((gx_size, 8, 128), f32),
                pltpu.VMEM((yz_size, 8, 128), f32),
                dma((X,)), dma((3, ring)),
                dma((3, MESSAGES)), dma((3, MESSAGES)),
                dma((3,)), dma((3,)),
                dma((gx_size - 1,)), dma((gx_size - 1,)),
                dma((yz_size - 1,)), dma((yz_size - 1,)),
            ],
            compiler_params=pltpu.CompilerParams(
                collective_id=0, has_side_effects=True, vmem_limit_bytes=50 * 1024 * 1024,
            ),
        )(right_side, viscosity, strain_rate, cell_code)

    placed = (
        P(None, "gx", "yz", None),
        P("gx", "yz", None),
        P(None, "gx", "yz", None),
        P("gx", "yz", None),
    )
    return jax.shard_map(
        per_device,
        mesh=mesh,
        in_specs=placed,
        out_specs=(P(None, "gx", "yz", None), P(None, "gx", "yz", None)),
        check_vma=False,
    )
```

```python
import functools

import jax
import jax.numpy as jnp
from jax import lax
from jax.experimental import pallas as pl
from jax.experimental.pallas import tpu as pltpu
from jax.sharding import PartitionSpec as P

SOFTEN = 0.8
ROWS = 8
PACKED = 16
RING = 4
UNROLL = 4
MESH = pl.DeviceIdType.MESH

UP_X, DOWN_X, UP_DIAG, DOWN_DIAG, UP_MID, DOWN_MID, UP_ENDS, DOWN_ENDS = range(8)
MESSAGES = 8
LATE = (1, 1, 2)
TURN = (1, 2, 3)


def softening(strain, eta):
    self_dot = (
        strain[0] * strain[0] + strain[1] * strain[1] + strain[2] * strain[2]
        + 2.0 * (strain[3] * strain[3] + strain[4] * strain[4] + strain[5] * strain[5])
    )
    return (2.0 * SOFTEN) * eta / (1.0 + self_dot)


def stress(base, next_x, next_y, next_z, strain, eta, soft):
    along_x = [next_x[c] - base[c] for c in range(3)]
    along_y = [next_y[c] - base[c] for c in range(3)]
    along_z = [next_z[c] - base[c] for c in range(3)]
    parts = [
        along_x[0], along_y[1], along_z[2],
        along_y[0] + along_x[1], along_z[0] + along_x[2], along_z[1] + along_y[2],
    ]
    cross = (
        (strain[0] * parts[0] + strain[1] * parts[1])
        + (strain[2] * parts[2] + strain[3] * parts[3])
        + (strain[4] * parts[4] + strain[5] * parts[5])
    )
    factor = soft * cross
    twice = eta + eta
    return [(twice if k < 3 else eta) * parts[k] - factor * strain[k] for k in range(6)]


def kernel(
    gx_size, yz_size,
    load, viscosity, strain_rate, code,
    field, resid,
    m0, m1, m2, strain, eta, soft, weight, flux,
    raw_s, raw_v, raw_c, edge_xs, edge_xv, edge_out, edge_in,
    mid_out, mid_in, ends_out, ends_in,
    sums_x, sums_y,
    load_sem, raw_sem, send_sem, recv_sem, edge_send, edge_recv,
    sum_send_x, sum_recv_x, sum_send_y, sum_recv_y,
):
    _, X, Y, Z = load.shape
    blocks = Y // ROWS
    gx = lax.axis_index("gx")
    yz = lax.axis_index("yz")
    low_x, high_x = gx == 0, gx == gx_size - 1
    low_y, high_y = yz == 0, yz == yz_size - 1
    not_ = jnp.logical_not
    both = jnp.logical_and
    above_x, below_x = lax.rem(gx + 1, gx_size), lax.rem(gx + gx_size - 1, gx_size)
    above_y, below_y = lax.rem(yz + 1, yz_size), lax.rem(yz + yz_size - 1, yz_size)
    ring = min(RING, X)

    def layer_of(i):
        return lax.rem(i + X - 1, X)

    def load_copy(x):
        return pltpu.make_async_copy(load.at[:, x], field.at[:, x], load_sem.at[x])

    def raw_copies(i):
        x, slot = layer_of(i), lax.rem(i, ring)
        return (
            pltpu.make_async_copy(strain_rate.at[:, x], raw_s.at[slot], raw_sem.at[0, slot]),
            pltpu.make_async_copy(viscosity.at[x], raw_v.at[slot], raw_sem.at[1, slot]),
            pltpu.make_async_copy(code.at[x], raw_c.at[slot], raw_sem.at[2, slot]),
        )

    for i in range(ring):
        for copy in raw_copies(jnp.int32(i)):
            copy.start()
        load_copy(layer_of(jnp.int32(i))).start()
    for i in range(ring, X):
        load_copy(layer_of(jnp.int32(i))).start()

    barrier = pltpu.get_barrier_semaphore()
    for k in range(1, gx_size):
        pl.semaphore_signal(barrier, inc=1, device_id=(lax.rem(gx + k, gx_size), yz), device_id_type=MESH)
    for k in range(1, yz_size):
        pl.semaphore_signal(barrier, inc=1, device_id=(gx, lax.rem(yz + k, yz_size)), device_id_type=MESH)
    has_up_diag = both(not_(high_x), not_(low_y))
    has_down_diag = both(not_(low_x), not_(high_y))

    for peer in ((above_x, below_y), (below_x, above_y)):
        pl.semaphore_signal(barrier, inc=1, device_id=peer, device_id_type=MESH)

    fields = (m0, m1, m2)

    @pl.when(low_x)
    def _():
        strain[:, 0, ROWS:] = jnp.zeros((6, Y, Z), jnp.float32)
        eta[0, ROWS:] = jnp.zeros((Y, Z), jnp.float32)
        soft[0, ROWS:] = jnp.zeros((Y, Z), jnp.float32)
        for m in fields:
            m[:, 0, ROWS:] = jnp.zeros((3, Y + ROWS, Z), jnp.float32)

    @pl.when(high_x)
    def _():
        for m in fields:
            m[:, X + 1] = jnp.zeros((3, Y + 2 * ROWS, Z), jnp.float32)

    @pl.when(low_y)
    def _():
        strain[:, 1:, :ROWS] = jnp.zeros((6, X, ROWS, Z), jnp.float32)
        eta[1:, :ROWS] = jnp.zeros((X, ROWS, Z), jnp.float32)
        soft[1:, :ROWS] = jnp.zeros((X, ROWS, Z), jnp.float32)
        for m in fields:
            m[:, 1:, :ROWS] = jnp.zeros((3, X + 1, ROWS, Z), jnp.float32)

    @pl.when(high_y)
    def _():
        for m in fields:
            m[:, :X + 1, Y + ROWS:] = jnp.zeros((3, X + 1, ROWS, Z), jnp.float32)

    def edge(i):
        src, dst, to = (
            (strain_rate.at[:, X - 1], edge_xs, (above_x, yz)),
            (viscosity.at[X - 1], edge_xv, (above_x, yz)),
            (edge_out, edge_in, (gx, above_y)),
        )[i]
        return pltpu.make_async_remote_copy(
            src_ref=src, dst_ref=dst, send_sem=edge_send.at[i], recv_sem=edge_recv.at[i],
            device_id=to, device_id_type=MESH,
        )

    sends = [not_(high_x), not_(low_x), has_up_diag, has_down_diag] + [not_(high_y), not_(low_y)] * 2
    recvs = [not_(low_x), not_(high_x), has_down_diag, has_up_diag] + [not_(low_y), not_(high_y)] * 2

    def message(step, i):
        m = fields[step]
        own = pl.ds(ROWS, Y)
        first, last = pl.ds(ROWS, ROWS), pl.ds(Y, ROWS)
        under, over = pl.ds(0, ROWS), pl.ds(Y + ROWS, ROWS)
        if i == UP_X:
            src, dst, to = m.at[:, X, own], m.at[:, 0, own], (above_x, yz)
        elif i == DOWN_X:
            src, dst, to = m.at[:, 1, own], m.at[:, X + 1, own], (below_x, yz)
        elif i == UP_DIAG:
            src, dst, to = m.at[:, X, first], m.at[:, 0, over], (above_x, below_y)
        elif i == DOWN_DIAG:
            src, dst, to = m.at[:, 1, last], m.at[:, X + 1, under], (below_x, above_y)
        else:
            way = (i - UP_MID) % 2
            there, here = (mid_out, mid_in) if i < UP_ENDS else (ends_out, ends_in)
            src, dst = there.at[step, way], here.at[step, way]
            to = (gx, below_y if way else above_y)
        return pltpu.make_async_remote_copy(
            src_ref=src, dst_ref=dst, send_sem=send_sem.at[step, i], recv_sem=recv_sem.at[step, i],
            device_id=to, device_id_type=MESH,
        )

    def send(step, which):
        for i in which:
            @pl.when(sends[i])
            def _(i=i):
                message(step, i).start()

    def receive(step, which):
        for i in which:
            @pl.when(recvs[i])
            def _(i=i):
                message(step, i).wait_recv()

    to_high = (UP_X, UP_DIAG)
    to_low = (DOWN_X, DOWN_DIAG)
    to_ends = (UP_ENDS, DOWN_ENDS)
    to_mid = (UP_MID, DOWN_MID)

    def stage(step, x):
        m = fields[step]
        inner = x > LATE[step]
        for way, at in enumerate((Y + ROWS - 1, ROWS)):
            line = [m[c, x, pl.ds(at, 1)] for c in range(3)]

            @pl.when(inner)
            def _(way=way, line=line):
                for c in range(3):
                    mid_out[step, way, c, pl.ds(x - 1, 1)] = line[c]

            @pl.when(not_(inner))
            def _(way=way, line=line):
                for c in range(3):
                    ends_out[step, way, pl.ds(3 * (x - 1) + c, 1)] = line[c]

    def spread(step, kind):
        m = fields[step]
        late = LATE[step]
        for way, at in enumerate((0, Y + ROWS)):
            @pl.when(recvs[kind + way])
            def _(way=way, at=at):
                message(step, kind + way).wait_recv()
                for c in range(3):
                    for x in range(late + 1, X + 1) if kind == UP_MID else range(1, late + 1):
                        if kind == UP_MID:
                            line = mid_in[step, way, c, pl.ds(x - 1, 1)]
                        else:
                            line = ends_in[step, way, pl.ds(3 * (x - 1) + c, 1)]
                        m[c, x, pl.ds(at, ROWS)] = jnp.broadcast_to(line, (ROWS, Z))

    zero = jnp.zeros((ROWS, Z), jnp.float32)

    def prepare(i, sums):
        x, slot = layer_of(i), lax.rem(i, ring)
        for copy in raw_copies(i):
            copy.wait()
        load_copy(x).wait()

        def body(j, sums):
            held, free = sums
            here = pl.ds(pl.multiple_of(j * PACKED, PACKED), PACKED)
            there = pl.ds(pl.multiple_of(j * PACKED + ROWS, ROWS), PACKED)
            s = [raw_s[slot, k, here].astype(jnp.float32) for k in range(6)]
            v = raw_v[slot, here].astype(jnp.float32)
            kind = raw_c[slot, here]
            pin = kind == 0
            for k in range(6):
                strain[k, x + 1, there] = s[k]
            eta[x + 1, there] = v
            soft[x + 1, there] = softening(s, v)
            weight[x, here] = jnp.where(pin, 0.0, jnp.where(kind == 1, 0.2, 1.2)).astype(jnp.float32)
            for c in range(3):
                b = field[c, x, here]
                m = jnp.where(pin, 0.0, b)
                p = jnp.where(pin, b, 0.0)
                m0[c, x + 1, there] = m
                m, p = m * m, p * p
                free = free + (m[:ROWS] + m[ROWS:])
                held = held + (p[:ROWS] + p[ROWS:])
            return held, free

        sums = lax.fori_loop(0, Y // PACKED, body, sums, unroll=UNROLL)

        stage(0, x + 1)
        at = pl.ds(Y + ROWS - 1, 1)
        for k in range(6):
            edge_out[k, pl.ds(x, 1)] = strain[k, x + 1, at]
        edge_out[6, pl.ds(x, 1)] = eta[x + 1, at]
        edge_out[7, pl.ds(x, 1)] = soft[x + 1, at]

        @pl.when(i + ring < X)
        def _():
            for copy in raw_copies(i + ring):
                copy.start()

        return sums

    sums = prepare(jnp.int32(0), (zero, zero))
    pl.semaphore_wait(barrier, gx_size - 1 + yz_size - 1 + 2)

    send(0, to_high)

    @pl.when(not_(high_x))
    def _():
        edge(0).start()
        edge(1).start()

    sums = prepare(jnp.int32(1), sums)
    send(0, to_low + to_ends)
    held, free = lax.fori_loop(2, X, prepare, sums)
    send(0, to_mid)

    @pl.when(not_(high_y))
    def _():
        edge(2).start()

    row = lax.broadcasted_iota(jnp.int32, (ROWS, Z), 0)
    lane = lax.broadcasted_iota(jnp.int32, (ROWS, Z), 1)
    top_row, bottom_row = row == 0, row == ROWS - 1
    first_lane, last_lane = lane == 0, lane == Z - 1

    def rows(j):
        return pl.ds(j * ROWS, ROWS)

    def tau(m, x, j, base, up):
        here = rows(j)
        next_x = [m[c, x + 1, here] for c in range(3)]
        next_y = [pltpu.roll(jnp.where(top_row, up[c], base[c]), ROWS - 1, 0) for c in range(3)]
        next_z = [jnp.where(last_lane, 0.0, pltpu.roll(base[c], Z - 1, 1)) for c in range(3)]
        s = [strain[k, x, here] for k in range(6)]
        return stress(base, next_x, next_y, next_z, s, eta[x, here], soft[x, here])

    def block(m, x, j):
        return tuple(m[c, x, rows(j)] for c in range(3))

    def flux_layer(m, x):
        base = block(m, x, 1)
        for j in range(1, blocks + 1):
            up = block(m, x, j + 1)
            t = tau(m, x, j, base, up)
            for c, k in enumerate((0, 3, 4)):
                flux[c, rows(j - 1)] = t[k]
            base = up

    def image_layer(m, out, shift, x, sums):
        one, two = sums
        base = block(m, x, 0)
        up = block(m, x, 1)
        t = tau(m, x, 0, base, up)
        base, prev = up, (t[3], t[1], t[5])
        for j in range(1, blocks + 1):
            up = block(m, x, j + 1)
            t = tau(m, x, j, base, up)
            fx, fy, fz = (t[0], t[3], t[4]), (t[3], t[1], t[5]), (t[4], t[5], t[2])
            w = weight[x - 1, rows(j - 1)]
            kept = w > 0.0
            for c in range(3):
                before_x = flux[c, rows(j - 1)]
                before_y = pltpu.roll(jnp.where(bottom_row, prev[c], fy[c]), 1, 0)
                before_z = jnp.where(first_lane, 0.0, pltpu.roll(fz[c], 1, 1))
                value = (before_x - fx[c]) + (before_y - fy[c]) + (before_z - fz[c]) + w * base[c]
                value = jnp.where(kept, value, 0.0)
                flux[c, rows(j - 1)] = fx[c]
                out[c, x - shift, rows(j - shift)] = value
                one = one + base[c] * value
                two = two + value * value
            base, prev = up, fy
        return one, two

    def edge_block(raw, shown, dst):
        s, v = raw
        s = [a.astype(jnp.float32)[shown] for a in s]
        v = v.astype(jnp.float32)[shown]
        x, at = dst
        for k in range(6):
            strain[k, x, at] = s[k]
        eta[x, at] = v
        soft[x, at] = softening(s, v)

    def coefficients_below():
        @pl.when(not_(low_x))
        def _():
            edge(0).wait_recv()
            edge(1).wait_recv()

            @pl.loop(0, Y // PACKED)
            def _(j):
                at = pl.ds(pl.multiple_of(j * PACKED, PACKED), PACKED)
                raw = [edge_xs[k, at] for k in range(6)], edge_xv[at]
                to = pl.ds(pl.multiple_of(j * PACKED + ROWS, ROWS), PACKED)
                edge_block(raw, slice(0, PACKED), (0, to))

    totals = [held, free]
    for step in range(3):
        m = fields[step]
        out, shift = (fields[step + 1], 0) if step < 2 else (resid, 1)
        spread(step, UP_MID)
        if step == 0:
            spread(step, UP_ENDS)

            @pl.when(not_(low_y))
            def _():
                edge(2).wait_recv()
                for x in range(X):
                    line = [jnp.broadcast_to(edge_in[k, pl.ds(x, 1)], (ROWS, Z)) for k in range(8)]
                    for k in range(6):
                        strain[k, x + 1, pl.ds(0, ROWS)] = line[k]
                    eta[x + 1, pl.ds(0, ROWS)] = line[6]
                    soft[x + 1, pl.ds(0, ROWS)] = line[7]

        def turn(t, sums, step=step, m=m, out=out, shift=shift):
            begin = TURN[step]
            x = lax.rem(t + begin, X) + 1

            @pl.when(t == X - begin - 1)
            def _():
                receive(step, (DOWN_X, DOWN_DIAG))

            @pl.when(t == X - begin)
            def _():
                if step < 2:
                    send(step + 1, to_high + to_mid)
                receive(step, (UP_X, UP_DIAG))
                if step == 0:
                    coefficients_below()
                else:
                    spread(step, UP_ENDS)

            @pl.when(jnp.logical_or(t == 0, t == X - begin))
            def _():
                flux_layer(m, x - 1)

            sums = image_layer(m, out, shift, x, sums)
            if step < 2:
                stage(step + 1, x)

                @pl.when(t == X - begin)
                def _():
                    send(step + 1, to_low)

            return sums

        sums = lax.fori_loop(0, X, turn, (zero, zero))
        if step < 2:
            send(step + 1, to_ends)
        totals += list(sums)

    totals = totals[:7]
    lines = [sum(jnp.sum(a, 0, keepdims=True)[:, k:k + 128] for k in range(0, Z, 128)) for a in totals]
    number = lax.broadcasted_iota(jnp.int32, (8, 128), 0)
    tile = jnp.zeros((8, 128), jnp.float32)
    for k, line in enumerate(lines):
        tile = jnp.where(number == k, jnp.broadcast_to(line, (8, 128)), tile)

    def exchange(buf, axis, me, size, send_s, recv_s, tile):
        buf[me] = tile

        def copy(k):
            peer = lax.rem(me + k, size)
            to = (peer, yz) if axis == 0 else (gx, peer)
            return pltpu.make_async_remote_copy(
                src_ref=buf.at[me], dst_ref=buf.at[me], send_sem=send_s.at[k - 1],
                recv_sem=recv_s.at[k - 1], device_id=to, device_id_type=MESH,
            )

        def arrival(k):
            peer = lax.rem(me + size - k, size)
            to = (peer, yz) if axis == 0 else (gx, peer)
            return pltpu.make_async_remote_copy(
                src_ref=buf.at[peer], dst_ref=buf.at[peer], send_sem=send_s.at[k - 1],
                recv_sem=recv_s.at[k - 1], device_id=to, device_id_type=MESH,
            )

        for k in range(1, size):
            copy(k).start()
        for k in range(1, size):
            arrival(k).wait_recv()
        total = buf[0]
        for k in range(1, size):
            total = total + buf[k]
        for k in range(1, size):
            copy(k).wait_send()
        return total

    tile = exchange(sums_x, 0, gx, gx_size, sum_send_x, sum_recv_x, tile)
    tile = exchange(sums_y, 1, yz, yz_size, sum_send_y, sum_recv_y, tile)
    tile = jnp.sum(tile, axis=1, keepdims=True)
    pinned = tile[0:1]
    mu = [tile[k:k + 1] + pinned for k in range(1, 7)]

    scale = mu[1] / mu[0]
    n, power = [], jnp.ones_like(scale)
    for k in range(6):
        n.append(mu[k] / mu[0] / power)
        power = power * scale
    a11, a12, a22 = n[3] - n[2] * n[2], n[4] - n[2] * n[3], n[5] - n[3] * n[3]
    y1, y2 = 1.0 - n[2], n[2] - n[3]
    ratio = a12 / a11
    c2 = (y2 - ratio * y1) / (a22 - ratio * a12)
    c1 = (y1 - a12 * c2) / a11
    c0 = 1.0 - n[2] * c1 - n[3] * c2
    c0, c1, c2 = [
        jnp.broadcast_to(c, (ROWS, Z))
        for c in (c0 / scale, c1 / scale / scale, c2 / scale / scale / scale)
    ]

    @pl.loop(0, X)
    def _(x):
        for j in range(blocks):
            here, there = rows(j), rows(j + 1)
            kept = weight[x, here] > 0.0
            for c in range(3):
                v0 = field[c, x, here]
                v1 = jnp.where(kept, m1[c, x + 1, there], v0)
                v2 = jnp.where(kept, m2[c, x + 1, there], v0)
                v3 = jnp.where(kept, resid[c, x, here], v0)
                field[c, x, here] = c0 * v0 + c1 * v1 + c2 * v2
                resid[c, x, here] = v0 - c0 * v1 - c1 * v2 - c2 * v3

    for step in range(3):
        for i in range(MESSAGES):
            @pl.when(sends[i])
            def _(step=step, i=i):
                message(step, i).wait_send()

    @pl.when(not_(high_x))
    def _():
        edge(0).wait_send()
        edge(1).wait_send()

    @pl.when(not_(high_y))
    def _():
        edge(2).wait_send()


def solution(mesh):
    gx_size, yz_size = mesh.shape["gx"], mesh.shape["yz"]

    def per_device(right_side, viscosity, strain_rate, cell_code):
        _, X, Y, Z = right_side.shape
        ring = min(RING, X)
        f32, bf16 = jnp.float32, jnp.bfloat16
        result = pltpu.VMEM(right_side.shape, f32)
        padded = pltpu.VMEM((3, X + 2, Y + 2 * ROWS, Z), f32)
        dma = pltpu.SemaphoreType.DMA
        return pl.pallas_call(
            functools.partial(kernel, gx_size, yz_size),
            out_shape=(result, result),
            in_specs=[pl.BlockSpec(memory_space=pl.ANY)] * 4,
            out_specs=(pl.BlockSpec(memory_space=pltpu.VMEM),) * 2,
            scratch_shapes=[
                padded, padded, padded,
                pltpu.VMEM((6, X + 1, Y + ROWS, Z), f32),
                pltpu.VMEM((X + 1, Y + ROWS, Z), f32),
                pltpu.VMEM((X + 1, Y + ROWS, Z), f32),
                pltpu.VMEM((X, Y, Z), f32),
                pltpu.VMEM((3, Y, Z), f32),
                pltpu.VMEM((ring, 6, Y, Z), bf16),
                pltpu.VMEM((ring, Y, Z), bf16),
                pltpu.VMEM((ring, Y, Z), jnp.int32),
                pltpu.VMEM((6, Y, Z), bf16),
                pltpu.VMEM((Y, Z), bf16),
                pltpu.VMEM((8, X, Z), f32), pltpu.VMEM((8, X, Z), f32),
                pltpu.VMEM((3, 2, 3, X, Z), f32), pltpu.VMEM((3, 2, 3, X, Z), f32),
                pltpu.VMEM((3, 2, 8, Z), f32), pltpu.VMEM((3, 2, 8, Z), f32),
                pltpu.VMEM((gx_size, 8, 128), f32),
                pltpu.VMEM((yz_size, 8, 128), f32),
                dma((X,)), dma((3, ring)),
                dma((3, MESSAGES)), dma((3, MESSAGES)),
                dma((3,)), dma((3,)),
                dma((gx_size - 1,)), dma((gx_size - 1,)),
                dma((yz_size - 1,)), dma((yz_size - 1,)),
            ],
            compiler_params=pltpu.CompilerParams(
                collective_id=0, has_side_effects=True, vmem_limit_bytes=50 * 1024 * 1024,
            ),
        )(right_side, viscosity, strain_rate, cell_code)

    placed = (
        P(None, "gx", "yz", None),
        P("gx", "yz", None),
        P(None, "gx", "yz", None),
        P("gx", "yz", None),
    )
    return jax.shard_map(
        per_device,
        mesh=mesh,
        in_specs=placed,
        out_specs=(P(None, "gx", "yz", None), P(None, "gx", "yz", None)),
        check_vma=False,
    )
```
